32 devices in a mesh: lat: 8 (over z, x), rad: 4 (over y, core).
Axes of the slice: x: 2, y: 2, z: 4, core: 2. Of those that a mesh axis runs over, the one named last changes fastest.
Arguments:
- kernels: float32 [3, 256000], P(None, 'lat'), may hold values from -6 to 6
- cells: int32 [3, 2048], P(None, 'lat'), may hold values from 0 to 251, as said below
- tiles: int32 [2048, 1], P('lat'), may hold values from 0 to 7; in each aligned block of 256 rows (0 to 255, 256 to 511, ...) at most 64 rows name the same one
- width_class: int32 [8], P('lat'), may hold values from 0 to 3
Outputs:
- smoothed: float32 [3, 64, 128, 256], P(None, 'lat', 'rad')
The draws below stay inside these ranges and needn't reach their ends.
Inputs may be any that keep to these rules, and one draw needn't show every extreme that they name: `tiles`: of the elements of one index of lat, at most 64 name the same tile, a bound that some block reaches of them. cells[0, e] <= 3, cells[1, e] <= 123 and cells[2, e] <= 251, so that each element's 5 x 5 x 5 block lies in its tile; each bound is reached.
All inputs are finite; a program needn't handle non-finite values.
Results may differ from the reference program's by a relative error of at most 0.000078.
Values sent between devices are 32-bit elements; how exact they have to be, the bound alone decides.
A program may use at most 192 MiB of HBM per device.

```python
import math
import jax
import jax.numpy as jnp
import numpy as np

CX = 8
NY = 256
E_DEV = 256
NGLL = 125
HW = 4
HY = 8
HZ = 4
NX = 64
NZ = 128
ELEMS = 2048
CAP = 64
N_LAT = 8


def draw_cells(key, part):
    key_x, key_y, key_z = jax.random.split(jax.random.fold_in(key, 11), 3)
    base_x = jax.random.randint(key_x, (ELEMS,), 0, CX - 4)
    base_y = jax.random.randint(key_y, (ELEMS,), 0, NY - 4)
    base_z = jax.random.randint(key_z, (ELEMS,), 0, NZ - 4)
    base_x = base_x.at[0].set(0).at[1].set(CX - 5)
    base_y = base_y.at[0].set(0).at[1].set(NY - 5)
    base_z = base_z.at[0].set(0).at[1].set(NZ - 5)
    return jnp.stack([base_x, base_z, base_y]).astype(jnp.int32)


def set_ends(values, key, least, top_value):
    longest = values.shape.index(max(values.shape))
    spots = []
    for shift in (0, 1):
        where = [jax.random.randint(jax.random.fold_in(key, axis), (), 0, length) for axis, length in enumerate(values.shape)]
        where[longest] = (where[longest] + shift) % values.shape[longest]
        spots.append(tuple(where))
    return values.at[spots[0]].set(least).at[spots[1]].set(top_value)


def shard_levels(rng, shape, cuts, smallest, top_value):
    def one(axis_at, parts):
        heights = jax.random.uniform(jax.random.fold_in(jax.random.fold_in(rng, 6), axis_at), (parts,), jnp.float32, smallest / len(cuts), top_value / len(cuts))
        return jnp.repeat(jnp.exp(heights), shape[axis_at] // parts).reshape((-1,) + (1,) * (len(shape) - axis_at - 1))

    level = one(*cuts[0])
    for cut in cuts[1:]:
        level = level * one(*cut)
    return level


def deal_out(rng, own, number, rows, count, top, limit, skew):
    sequence = jax.random.permutation(rng, count)
    packed, common = load_shares(count, rows * top, limit, skew, True), load_shares(count, rows * top, limit, skew, False)
    places = jnp.arange(count)

    def named(sizes, rotation):
        used = int((sizes > 0).sum())
        fixed = max(1, used // 4)
        shifted = fixed + (places - fixed + rotation * (used - fixed)) % max(1, count - fixed)
        return jnp.zeros((count,), jnp.int32).at[sequence[jnp.where(places < fixed, places, shifted)]].set(jnp.asarray(sizes, jnp.int32))

    sizes = jnp.where(number % 4 == 0, named(packed, number // 4), named(common, number - number // 4 - 1))
    mixed = jax.random.permutation(jax.random.fold_in(own, 3), count)
    source_of, sink = mixed[0:count // 2 * 2:2], mixed[1:count // 2 * 2:2]
    room = jnp.minimum(sizes[source_of] - 1, limit - sizes[sink]) // 2
    room = jnp.where((source_of == sequence[0]) | (sink == sequence[0]) | (sizes[sink] == 0), 0, jnp.maximum(room, 0))
    shifted = jax.random.randint(jax.random.fold_in(own, 4), (count // 2,), 0, 1 << 20) % (room + 1)
    sizes = sizes.at[source_of].add(-shifted).at[sink].add(shifted)
    members = jnp.searchsorted(jnp.cumsum(sizes), jnp.arange(rows * top), side="right").astype(jnp.int32)
    table = members.reshape(top, rows).T
    table = table[jax.random.permutation(jax.random.fold_in(own, 1), rows)]
    rotation = jax.random.randint(jax.random.fold_in(own, 2), (rows, 1), 0, top)
    return jnp.take_along_axis(table, (jnp.arange(top)[None, :] + rotation) % top, axis=1)


def load_shares(number_of, total, most, lean, full):
    weights = [(1 << 20) // math.isqrt(standing ** lean) + 1 for standing in range(1, number_of + 1)]
    largest = most if full else min(most, max(-(-total // number_of), total * weights[0] // sum(weights)))
    least = 1 if total - largest >= number_of - 1 else 0
    counts, spare = [largest] + [least] * (number_of - 1), total - largest - least * (number_of - 1)
    while spare > 0:
        movable = [i for i in range(1, number_of) if counts[i] < largest] or [i for i in range(1, number_of) if counts[i] < most]
        whole, left = sum([weights[i] for i in movable]), spare
        for i in movable:
            more = min(most - counts[i], max(1, left * weights[i] // whole), spare)
            counts[i] = counts[i] + more
            spare = spare - more
    return np.array(counts)


def bell_draw(stream_key, dims, width, limit, cuts=(), held_as=jnp.bfloat16):
    values = width * jax.random.normal(stream_key, dims, jnp.float32)
    if cuts:
        values = values * shard_levels(stream_key, dims, cuts, -0.22, 0.18)
    return jnp.clip(values, -limit, limit).astype(held_as)


def setup_inputs(seed: int = 0) -> dict:
    key_list = jax.random.split(jax.random.key(seed), 5)
    kernels = bell_draw(key_list[0], (3, ELEMS * NGLL), 1.0, 6.0, ((1, 8),), jnp.float32)
    cells = draw_cells(jax.random.fold_in(key_list[4], 71), 0)
    tiles_keys = jax.random.split(jax.random.fold_in(key_list[2], 1), ELEMS // E_DEV)
    tiles_turns = jax.random.permutation(jax.random.fold_in(key_list[2], 3), ELEMS // E_DEV)
    tiles = jax.vmap(lambda own, number: deal_out(jax.random.fold_in(key_list[2], 2), own, number, E_DEV, N_LAT, 1, CAP, 2))(tiles_keys, tiles_turns).reshape((ELEMS, 1))
    width_class = set_ends(jax.random.randint(key_list[3], (N_LAT,), 0, 4), jax.random.fold_in(key_list[3], 1), 0, 3).astype(jnp.int32)
    return {"kernels": kernels, "cells": cells, "tiles": tiles, "width_class": width_class}


def band_weights(count, sigma, half):
    place = jnp.arange(count)
    offsets = jnp.arange(-half, half + 1)
    target = place[:, None] + offsets[None, :]
    valid = (target >= 0) & (target < count)
    gauss = jnp.exp(-(offsets[None, :].astype(jnp.float32) ** 2) / (2.0 * sigma[:, None] ** 2))
    gauss = jnp.where(valid, gauss, jnp.float32(0.0))
    return gauss / jnp.sum(gauss, axis=1, keepdims=True)


def lax_slice(array, axis, start, length):
    return jax.lax.slice_in_dim(array, start, start + length, axis=axis)


def band_apply(field, weights, axis, half):
    count = field.shape[axis]
    widths = [(0, 0)] * field.ndim
    widths[axis] = (half, half)
    padded = jnp.pad(field, widths)
    shape = [1] * field.ndim
    shape[axis] = count
    total = jnp.zeros_like(field)
    for offset in range(-half, half + 1):
        piece = lax_slice(padded, axis, half + offset, count)
        total = total + weights[:, offset + half].reshape(shape) * piece
    return total


def point_cells(cells, depth):
    points = jnp.arange(NGLL, dtype=jnp.int32)
    along_x = points // 25
    along_z = (points // 5) % 5
    along_y = points % 5
    return (cells[0][:, None] + along_x[None, :]) * (depth * NY) + (cells[1][:, None] + along_z[None, :]) * NY + (cells[2][:, None] + along_y[None, :])


def reference(kernels, cells, tiles, width_class):
    flat = point_cells(cells, NZ)
    global_cells = (tiles[:, 0][:, None] * (CX * NZ * NY) + flat).reshape(-1)
    summed = jnp.zeros((3, NX * NZ * NY), jnp.float32).at[:, global_cells].add(kernels)
    summed = summed.reshape(3, NX, NZ, NY)
    sigma_x = 1.0 + 0.75 * width_class[jnp.arange(NX) // CX].astype(jnp.float32)
    lateral = band_apply(summed, band_weights(NX, sigma_x, HW), 1, HW)
    across = band_apply(lateral, band_weights(NY, jnp.full((NY,), 2.5, jnp.float32), HY), 3, HY)
    return band_apply(across, band_weights(NZ, jnp.full((NZ,), 1.5, jnp.float32), HZ), 2, HZ)
```

```python
import functools

import jax
import jax.numpy as jnp
import numpy as np
from jax import lax
from jax.experimental import pallas as pl
from jax.experimental.pallas import tpu as pltpu
from jax.sharding import PartitionSpec as P

CX = 8
NY = 256
CZ = 32
NGLL = 125
HW = 4
HY = 8
HZ = 4
ZP = CZ + 4 * HZ
LANES = 128
VMEM_LIMIT = 48 * 2**20


def band_matrix(count, sigma, half):
    place = np.arange(count)
    gap = place[None, :] - place[:, None]
    gauss = np.where(np.abs(gap) <= half, np.exp(-(gap**2) / (2.0 * sigma**2)), 0.0)
    return gauss / gauss.sum(axis=1, keepdims=True)


def z_matrices(n_rad):
    depth = CZ * n_rad
    padded = np.pad(band_matrix(depth, 1.5, HZ), ((0, 0), (HZ, HZ)))
    return np.stack(
        [padded[r * CZ : (r + 1) * CZ, r * CZ : (r + 1) * CZ + 2 * HZ] for r in range(n_rad)]
    ).astype(np.float32)


def pack_kernel(n_lat, cap, elements, tiles_ref, cells_ref, kern_ref, out_ref, count):
    rows = elements * NGLL // LANES
    out_ref[...] = jnp.full(out_ref.shape, -1000.0, jnp.float32)
    lane = lax.broadcasted_iota(jnp.int32, (3, LANES), 1)

    @pl.loop(0, n_lat)
    def _(t):
        count[t] = 0

    @pl.loop(0, elements)
    def _(e):
        t = tiles_ref[e]
        rank = count[t]
        count[t] = rank + 1
        start = e * NGLL
        row = start // LANES
        off = start - row * LANES
        after = jnp.minimum(row + 1, rows - 1)
        a = kern_ref[:, pl.ds(pl.multiple_of(row * LANES, LANES), LANES)]
        b = kern_ref[:, pl.ds(pl.multiple_of(after * LANES, LANES), LANES)]
        back = lax.rem(LANES - off, LANES)
        v = pltpu.roll(jnp.where(lane >= off, a, b), back, 1)
        x0 = cells_ref[e].astype(jnp.float32)
        z0 = cells_ref[elements + e].astype(jnp.float32)
        y0 = cells_ref[2 * elements + e].astype(jnp.float32)
        v = jnp.where(lane == NGLL, x0, v)
        v = jnp.where(lane == NGLL + 1, z0, v)
        v = jnp.where(lane == NGLL + 2, y0, v)
        base = t * (3 * cap) + rank
        for c in range(3):
            out_ref[pl.ds(base + c * cap, 1), :] = v[c : c + 1]


def sum_kernel(n_lat, cap, meta_ref, recv_ref, wz_ref, wy_ref, out_ref, acc):
    slab = lax.axis_index("rad")
    slots = n_lat * cap
    acc[...] = jnp.zeros(acc.shape, jnp.float32)
    lane = lax.broadcasted_iota(jnp.int32, (8, LANES), 1)

    @pl.loop(0, slots)
    def _(s):
        z0 = meta_ref[slots + s]
        zb = z0 - slab * CZ + 2 * HZ

        @pl.when((z0 >= 0) & (zb >= 0) & (zb < CZ + 3 * HZ))
        def _():
            x0 = meta_ref[s]
            y0 = meta_ref[2 * slots + s]
            src = s // cap
            base = src * (3 * cap) + (s - src * cap)
            v = jnp.concatenate(
                [recv_ref[pl.ds(base + c * cap, 1), :] for c in range(3)]
                + [jnp.zeros((5, LANES), jnp.float32)],
                axis=0,
            )
            yt = y0 // LANES
            yl = y0 - yt * LANES
            first = (lane >= yl) & (lane < yl + 5)

            def add(tile, mask):
                at = ((tile * CX + x0) * ZP + zb) * 8
                for i in range(5):
                    for j in range(5):
                        turn = lax.rem(yl + 2 * LANES - 5 * (5 * i + j), LANES)
                        piece = jnp.where(mask, pltpu.roll(v, turn, 1), 0.0)
                        row = pl.ds(pl.multiple_of(at + (i * ZP + j) * 8, 8), 8)
                        acc[row, :] += piece

            add(yt, first)

            @pl.when(yl > LANES - 5)
            def _():
                add(yt + 1, lane < yl + 5 - LANES)

    wz = wz_ref[slab]
    wy = wy_ref[...]
    for c in range(3):

        @pl.loop(0, CX)
        def _(x):
            halves = []
            for yt in range(NY // LANES):
                at = ((yt * CX + x) * ZP + HZ) * 8 + c
                halves.append(acc[pl.ds(at, CZ + 2 * HZ, stride=8), :])
            plane = jnp.concatenate(halves, axis=1)
            plane = jnp.dot(wz, plane, precision=lax.Precision.HIGHEST)
            plane = jnp.dot(plane, wy, precision=lax.Precision.HIGHEST)
            out_ref[c, x] = plane


def x_weights(width_class, n_lat):
    rows = lax.axis_index("lat") * CX + jnp.arange(CX)
    sigma = 1.0 + 0.75 * width_class[0].astype(jnp.float32)
    offsets = jnp.arange(-HW, HW + 1)
    target = rows[:, None] + offsets[None, :]
    valid = (target >= 0) & (target < CX * n_lat)
    gauss = jnp.exp(-(offsets[None, :].astype(jnp.float32) ** 2) / (2.0 * sigma**2))
    gauss = jnp.where(valid, gauss, 0.0)
    return gauss / jnp.sum(gauss, axis=1, keepdims=True)


def on_device(n_lat, n_rad, kernels, cells, tiles, width_class):
    elements = tiles.shape[0]
    cap = max(2, 2 * elements // n_lat)
    slots = n_lat * cap
    params = pltpu.CompilerParams(vmem_limit_bytes=VMEM_LIMIT)
    smem = pl.BlockSpec(memory_space=pltpu.SMEM)
    vmem = pl.BlockSpec(memory_space=pltpu.VMEM)
    send = pl.pallas_call(
        functools.partial(pack_kernel, n_lat, cap, elements),
        out_shape=jax.ShapeDtypeStruct((slots * 3, LANES), jnp.float32),
        in_specs=[smem, smem, vmem],
        out_specs=vmem,
        scratch_shapes=[pltpu.SMEM((n_lat,), jnp.int32)],
        compiler_params=params,
    )(tiles.reshape(-1), cells.reshape(-1), kernels)
    recv = lax.all_to_all(
        send.reshape(n_lat, 3 * cap, LANES), "lat", split_axis=0, concat_axis=0, tiled=True
    )
    meta = recv.reshape(n_lat, 3, cap, LANES)[:, 0, :, NGLL:]
    meta = meta.transpose(2, 0, 1).reshape(-1).astype(jnp.int32)
    part = pl.pallas_call(
        functools.partial(sum_kernel, n_lat, cap),
        out_shape=jax.ShapeDtypeStruct((3, CX, CZ, NY), jnp.float32),
        in_specs=[smem, vmem, vmem, vmem],
        out_specs=vmem,
        scratch_shapes=[pltpu.VMEM((NY // LANES * CX * ZP * 8, LANES), jnp.float32)],
        compiler_params=params,
    )(
        meta,
        recv.reshape(slots * 3, LANES),
        jnp.asarray(z_matrices(n_rad)),
        jnp.asarray(band_matrix(NY, 2.5, HY).T.astype(np.float32)),
    )
    up = [(i, i + 1) for i in range(n_lat - 1)]
    down = [(j, i) for i, j in up]
    before = lax.ppermute(part[:, CX - HW :], "lat", up)
    after = lax.ppermute(part[:, :HW], "lat", down)
    padded = jnp.concatenate([before, part, after], axis=1)
    weights = x_weights(width_class, n_lat)
    total = jnp.zeros_like(part)
    for d in range(2 * HW + 1):
        total = total + weights[:, d][None, :, None, None] * padded[:, d : d + CX]
    return total


def solution(mesh):
    return jax.shard_map(
        functools.partial(on_device, mesh.shape["lat"], mesh.shape["rad"]),
        mesh=mesh,
        in_specs=(P(None, "lat"), P(None, "lat"), P("lat", None), P("lat")),
        out_specs=P(None, "lat", "rad", None),
        check_vma=False,
    )
```

```python
import functools

import jax
import jax.numpy as jnp
import numpy as np
from jax import lax
from jax.experimental import pallas as pl
from jax.experimental.pallas import tpu as pltpu
from jax.sharding import PartitionSpec as P

CX = 8
NY = 256
CZ = 32
NGLL = 125
HW = 4
HY = 8
HZ = 4
ZP = CZ + 4 * HZ
LANES = 128
TAPS = 2 * HZ + 1
PACK_UNROLL = 4
SUM_UNROLL = 2
VMEM_LIMIT = 48 * 2**20
MESH = pl.DeviceIdType.MESH


def band_matrix(count, sigma, half):
    place = np.arange(count)
    gap = place[None, :] - place[:, None]
    gauss = np.where(np.abs(gap) <= half, np.exp(-(gap**2) / (2.0 * sigma**2)), 0.0)
    return gauss / gauss.sum(axis=1, keepdims=True)


def z_taps(n_rad):
    full = np.pad(band_matrix(CZ * n_rad, 1.5, HZ), ((0, 0), (HZ, HZ)))
    return np.stack([full[z, z : z + TAPS] for z in range(CZ * n_rad)]).astype(np.float32)


def pack_kernel(n_lat, n_rad, share, elements, tiles_ref, cells_ref, kern_ref, out_ref, count, todo, place):
    slab = lax.axis_index("rad")
    rows = elements * NGLL // LANES
    out_ref[...] = jnp.full(out_ref.shape, -1000.0, jnp.float32)
    lane = lax.broadcasted_iota(jnp.int32, (3, LANES), 1)

    @pl.loop(0, n_lat)
    def _(t):
        count[t] = 0

    def listed(e, n):
        t = tiles_ref[e]
        rank = count[t]
        count[t] = rank + 1
        slot = lax.div(rank, n_rad)
        todo[n] = e
        place[n] = t * share + slot
        return n + jnp.where(rank - slot * n_rad == slab, 1, 0)

    n = lax.fori_loop(0, elements, listed, 0, unroll=4)
    for more in range(PACK_UNROLL):
        todo[n + more] = 0
        place[n + more] = n_lat * share

    def packed(step, _):
        for u in range(PACK_UNROLL):
            e = todo[step * PACK_UNROLL + u]
            at = place[step * PACK_UNROLL + u]
            start = e * NGLL
            row = lax.shift_right_logical(start, 7)
            off = start & (LANES - 1)
            after = jnp.minimum(row + 1, rows - 1)
            a = kern_ref[:, pl.ds(pl.multiple_of(row * LANES, LANES), LANES)]
            b = kern_ref[:, pl.ds(pl.multiple_of(after * LANES, LANES), LANES)]
            v = pltpu.roll(jnp.where(lane >= off, a, b), (LANES - off) & (LANES - 1), 1)
            v = jnp.where(lane == NGLL, cells_ref[e].astype(jnp.float32), v)
            v = jnp.where(lane == NGLL + 1, cells_ref[elements + e].astype(jnp.float32), v)
            v = jnp.where(lane == NGLL + 2, cells_ref[2 * elements + e].astype(jnp.float32), v)
            t = lax.div(at, share)
            slot = at - t * share
            for c in range(3):
                out_ref[t, pl.ds(c * share + slot, 1), :] = v[c : c + 1]
        return 0

    lax.fori_loop(0, lax.div(n + PACK_UNROLL - 1, PACK_UNROLL), packed, 0)


def exchange_kernel(n_lat, n_rad, send_ref, recv_ref, own_sem, send_sem, recv_sem, fwd_sem, got_sem):
    tile, slab = lax.axis_index("lat"), lax.axis_index("rad")
    barrier = pltpu.get_barrier_semaphore()

    @pl.loop(1, n_lat)
    def _(k):
        pl.semaphore_signal(barrier, inc=1, device_id=(lax.rem(tile + k, n_lat), slab), device_id_type=MESH)

    for k in range(1, n_rad):
        pl.semaphore_signal(barrier, inc=1, device_id=(tile, lax.rem(slab + k, n_rad)), device_id_type=MESH)
    pl.semaphore_wait(barrier, n_lat - 1 + n_rad - 1)

    def across(k):
        to = lax.rem(tile + k, n_lat)
        return pltpu.make_async_remote_copy(
            src_ref=send_ref.at[to],
            dst_ref=recv_ref.at[slab, tile],
            send_sem=send_sem.at[k],
            recv_sem=recv_sem.at[k],
            device_id=(to, slab),
            device_id_type=MESH,
        )

    def forward(k, r):
        source = lax.rem(tile + n_lat - k, n_lat)
        block = recv_ref.at[slab, source]
        return pltpu.make_async_remote_copy(
            src_ref=block,
            dst_ref=block,
            send_sem=fwd_sem.at[r, k],
            recv_sem=got_sem.at[r, k],
            device_id=(tile, lax.rem(slab + r, n_rad)),
            device_id_type=MESH,
        )

    def arrived(k, r):
        source = lax.rem(tile + n_lat - k, n_lat)
        block = recv_ref.at[lax.rem(slab + n_rad - r, n_rad), source]
        return pltpu.make_async_remote_copy(
            src_ref=block,
            dst_ref=block,
            send_sem=fwd_sem.at[r, k],
            recv_sem=got_sem.at[r, k],
            device_id=(tile, lax.rem(slab + r, n_rad)),
            device_id_type=MESH,
        )

    @pl.loop(1, n_lat)
    def _(k):
        across(k).start()

    own = pltpu.make_async_copy(send_ref.at[tile], recv_ref.at[slab, tile], own_sem)
    own.start()
    own.wait()
    for r in range(1, n_rad):
        forward(0, r).start()

    @pl.loop(1, n_lat)
    def _(k):
        across(k).wait_recv()
        for r in range(1, n_rad):
            forward(k, r).start()

    @pl.loop(0, n_lat)
    def _(k):
        for r in range(1, n_rad):
            arrived(k, r).wait_recv()

    @pl.loop(1, n_lat)
    def _(k):
        across(k).wait_send()

    @pl.loop(0, n_lat)
    def _(k):
        for r in range(1, n_rad):
            forward(k, r).wait_send()


def sum_kernel(blocks, share, meta_ref, taps_ref, recv_ref, wy_ref, out_ref, acc, planes, todo):
    slab = lax.axis_index("rad")
    slots = blocks * share
    acc[...] = jnp.zeros(acc.shape, jnp.float32)
    lane = lax.broadcasted_iota(jnp.int32, (8, LANES), 1)
    sub = lax.broadcasted_iota(jnp.int32, (8, LANES), 0)
    ramp = 25 * sub + lane
    low = slab * CZ - 2 * HZ

    def listed(s, n):
        zb = meta_ref[slots + s] - low
        todo[n] = s
        return n + jnp.where((zb >= 0) & (zb < CZ + 3 * HZ), 1, 0)

    n = lax.fori_loop(0, slots, listed, 0, unroll=8)
    for more in range(SUM_UNROLL):
        todo[n + more] = 0

    def place(at, values, index, mask):
        for j in range(5):
            picked = jnp.where(mask, index + 5 * j, NGLL)
            for c in range(3):
                piece = jnp.take_along_axis(values[c], picked, axis=1, mode="promise_in_bounds")
                acc[pl.ds(pl.multiple_of(at + (3 * j + c) * 8, 8), 8), :] += piece

    def summed(step, _):
        later = []
        for u in range(SUM_UNROLL):
            s = todo[step * SUM_UNROLL + u]
            good = step * SUM_UNROLL + u < n
            x0 = jnp.clip(meta_ref[s], 0, CX - 5)
            zb = jnp.clip(meta_ref[slots + s] - low, 0, CZ + 3 * HZ - 1)
            y0 = jnp.clip(meta_ref[2 * slots + s], 0, NY - 5)
            block = lax.div(s, share)
            slot = s - block * share
            values = []
            for c in range(3):
                row = jnp.broadcast_to(recv_ref[block, pl.ds(c * share + slot, 1), :], (8, LANES))
                values.append(jnp.where(lane < NGLL, row, 0.0))
            half = lax.shift_right_logical(y0, 7)
            yl = y0 & (LANES - 1)
            index = ramp - (25 * x0 + yl)
            rows = (sub >= x0) & (sub < jnp.where(good, x0 + 5, 0))
            at = (half * ZP + zb) * 24
            place(at, values, index, rows & (lane >= yl) & (lane < yl + 5))
            later.append((at, values, index, rows, yl))
        for at, values, index, rows, yl in later:

            @pl.when(yl > LANES - 5)
            def _():
                over = rows & (lane < yl + 5 - LANES)
                place(at + ZP * 24, values, index + LANES, over)

        return 0

    lax.fori_loop(0, lax.div(n + SUM_UNROLL - 1, SUM_UNROLL), summed, 0)

    @pl.loop(0, CZ)
    def _(z):
        for half in range(NY // LANES):
            total = jnp.zeros((24, LANES), jnp.float32)
            for d in range(TAPS):
                weight = taps_ref[(slab * CZ + z) * TAPS + d]
                at = pl.multiple_of((half * ZP + z + HZ + d) * 24, 8)
                total = total + weight * acc[pl.ds(at, 24), :]
            planes[pl.ds(pl.multiple_of(z * 24, 8), 24), half * LANES : (half + 1) * LANES] = total

    step = CZ // 4
    for part in range(4):
        rows = slice(part * step * 24, (part + 1) * step * 24)
        product = jnp.dot(planes[rows, :], wy_ref[...], precision=lax.Precision.HIGHEST)
        for zz in range(step):
            for c in range(3):
                piece = product[zz * 24 + c * 8 : zz * 24 + c * 8 + 8]
                for half in range(NY // LANES):
                    cols = slice(half * LANES, (half + 1) * LANES)
                    out_ref[half, pl.ds(c * CX * CZ + part * step + zz, CX, stride=CZ), :] = piece[:, cols]


def x_weights(width_class, n_lat):
    rows = lax.axis_index("lat") * CX + jnp.arange(CX)
    sigma = 1.0 + 0.75 * width_class[0].astype(jnp.float32)
    offsets = jnp.arange(-HW, HW + 1)
    target = rows[:, None] + offsets[None, :]
    valid = (target >= 0) & (target < CX * n_lat)
    gauss = jnp.exp(-(offsets[None, :].astype(jnp.float32) ** 2) / (2.0 * sigma**2))
    gauss = jnp.where(valid, gauss, 0.0)
    return gauss / jnp.sum(gauss, axis=1, keepdims=True)


def on_device(n_lat, n_rad, kernels, cells, tiles, width_class):
    elements = tiles.shape[0]
    cap = max(2, 2 * elements // n_lat)
    share = -(-cap // n_rad)
    blocks = n_rad * n_lat
    slots = blocks * share
    params = pltpu.CompilerParams(vmem_limit_bytes=VMEM_LIMIT)
    smem = pl.BlockSpec(memory_space=pltpu.SMEM)
    vmem = pl.BlockSpec(memory_space=pltpu.VMEM)
    send = pl.pallas_call(
        functools.partial(pack_kernel, n_lat, n_rad, share, elements),
        out_shape=jax.ShapeDtypeStruct((n_lat + 1, 3 * share, LANES), jnp.float32),
        in_specs=[smem, smem, vmem],
        out_specs=vmem,
        scratch_shapes=[
            pltpu.SMEM((n_lat,), jnp.int32),
            pltpu.SMEM((elements + PACK_UNROLL,), jnp.int32),
            pltpu.SMEM((elements + PACK_UNROLL,), jnp.int32),
        ],
        compiler_params=params,
    )(tiles.reshape(-1), cells.reshape(-1), kernels)
    recv = pl.pallas_call(
        functools.partial(exchange_kernel, n_lat, n_rad),
        out_shape=jax.ShapeDtypeStruct((n_rad, n_lat, 3 * share, LANES), jnp.float32),
        in_specs=[vmem],
        out_specs=vmem,
        scratch_shapes=[
            pltpu.SemaphoreType.DMA,
            pltpu.SemaphoreType.DMA((n_lat,)),
            pltpu.SemaphoreType.DMA((n_lat,)),
            pltpu.SemaphoreType.DMA((n_rad, n_lat)),
            pltpu.SemaphoreType.DMA((n_rad, n_lat)),
        ],
        compiler_params=pltpu.CompilerParams(
            vmem_limit_bytes=VMEM_LIMIT, collective_id=0, has_side_effects=True
        ),
    )(send)
    recv = recv.reshape(blocks, 3 * share, LANES)
    meta = recv[:, :share, NGLL:].transpose(2, 0, 1).reshape(-1).astype(jnp.int32)
    part = pl.pallas_call(
        functools.partial(sum_kernel, blocks, share),
        out_shape=jax.ShapeDtypeStruct((NY // LANES, 3 * CX * CZ, LANES), jnp.float32),
        in_specs=[smem, smem, vmem, vmem],
        out_specs=vmem,
        scratch_shapes=[
            pltpu.VMEM((NY // LANES * ZP * 24, LANES), jnp.float32),
            pltpu.VMEM((CZ * 24, NY), jnp.float32),
            pltpu.SMEM((slots + SUM_UNROLL,), jnp.int32),
        ],
        compiler_params=params,
    )(
        meta,
        jnp.asarray(z_taps(n_rad).reshape(-1)),
        recv,
        jnp.asarray(band_matrix(NY, 2.5, HY).T.astype(np.float32)),
    )
    part = part.reshape(NY // LANES, 3, CX, CZ, LANES)
    up = [(i, i + 1) for i in range(n_lat - 1)]
    down = [(j, i) for i, j in up]
    before = lax.ppermute(part[:, :, CX - HW :], "lat", up)
    after = lax.ppermute(part[:, :, :HW], "lat", down)
    padded = jnp.concatenate([before, part, after], axis=2)
    weights = x_weights(width_class, n_lat)
    total = jnp.zeros_like(part)
    for d in range(2 * HW + 1):
        total = total + weights[:, d][None, None, :, None, None] * padded[:, :, d : d + CX]
    return total.transpose(1, 2, 3, 0, 4).reshape(3, CX, CZ, NY)


def solution(mesh):
    return jax.shard_map(
        functools.partial(on_device, mesh.shape["lat"], mesh.shape["rad"]),
        mesh=mesh,
        in_specs=(P(None, "lat"), P(None, "lat"), P("lat", None), P("lat")),
        out_specs=P(None, "lat", "rad", None),
        check_vma=False,
    )
```

```python
import functools

import jax
import jax.numpy as jnp
import numpy as np
from jax import lax
from jax.experimental import pallas as pl
from jax.experimental.pallas import tpu as pltpu
from jax.sharding import PartitionSpec as P

CX = 8
NY = 256
CZ = 32
NGLL = 125
HW = 4
HY = 8
HZ = 4
ZP = CZ + 4 * HZ
LANES = 128
TAPS = 2 * HZ + 1
PADX = CX + 2 * HW
PACK_UNROLL = 4
SUM_UNROLL = 4
VMEM_LIMIT = 48 * 2**20
MESH = pl.DeviceIdType.MESH


def band_matrix(count, sigma, half):
    place = np.arange(count)
    gap = place[None, :] - place[:, None]
    gauss = np.where(np.abs(gap) <= half, np.exp(-(gap**2) / (2.0 * sigma**2)), 0.0)
    return gauss / gauss.sum(axis=1, keepdims=True)


def z_taps(n_rad):
    full = np.pad(band_matrix(CZ * n_rad, 1.5, HZ), ((0, 0), (HZ, HZ)))
    return np.stack([full[z, z : z + TAPS] for z in range(CZ * n_rad)]).astype(np.float32)


def pack_kernel(n_lat, n_rad, share, elements, tiles_ref, cells_ref, kern_ref, out_ref, count, todo, place):
    slab = lax.axis_index("rad")
    rows = elements * NGLL // LANES
    out_ref[...] = jnp.full(out_ref.shape, -1000.0, jnp.float32)
    lane = lax.broadcasted_iota(jnp.int32, (3, LANES), 1)

    @pl.loop(0, n_lat)
    def _(t):
        count[t] = 0

    def listed(e, n):
        t = tiles_ref[e]
        rank = count[t]
        count[t] = rank + 1
        slot = lax.div(rank, n_rad)
        todo[n] = e
        place[n] = t * share + slot
        return n + jnp.where(rank - slot * n_rad == slab, 1, 0)

    n = lax.fori_loop(0, elements, listed, 0, unroll=4)
    for more in range(PACK_UNROLL):
        todo[n + more] = 0
        place[n + more] = n_lat * share

    def packed(step, _):
        for u in range(PACK_UNROLL):
            e = todo[step * PACK_UNROLL + u]
            at = place[step * PACK_UNROLL + u]
            start = e * NGLL
            row = lax.shift_right_logical(start, 7)
            off = start & (LANES - 1)
            after = jnp.minimum(row + 1, rows - 1)
            a = kern_ref[:, pl.ds(pl.multiple_of(row * LANES, LANES), LANES)]
            b = kern_ref[:, pl.ds(pl.multiple_of(after * LANES, LANES), LANES)]
            v = pltpu.roll(jnp.where(lane >= off, a, b), (LANES - off) & (LANES - 1), 1)
            v = jnp.where(lane == NGLL, cells_ref[0, e].astype(jnp.float32), v)
            v = jnp.where(lane == NGLL + 1, cells_ref[1, e].astype(jnp.float32), v)
            v = jnp.where(lane == NGLL + 2, cells_ref[2, e].astype(jnp.float32), v)
            t = lax.div(at, share)
            slot = at - t * share
            for c in range(3):
                out_ref[t, pl.ds(c * share + slot, 1), :] = v[c : c + 1]
        return 0

    lax.fori_loop(0, lax.div(n + PACK_UNROLL - 1, PACK_UNROLL), packed, 0)


def exchange_kernel(n_lat, n_rad, send_ref, recv_ref, own_sem, send_sem, recv_sem, fwd_sem, got_sem):
    tile, slab = lax.axis_index("lat"), lax.axis_index("rad")
    barrier = pltpu.get_barrier_semaphore()

    @pl.loop(1, n_lat)
    def _(k):
        pl.semaphore_signal(barrier, inc=1, device_id=(lax.rem(tile + k, n_lat), slab), device_id_type=MESH)

    pair = slab + 1 - 2 * lax.rem(slab, 2)
    other = slab + 2 - 4 * lax.div(slab, 2)
    for peer in (pair, other):
        pl.semaphore_signal(barrier, inc=1, device_id=(tile, peer), device_id_type=MESH)
    pl.semaphore_wait(barrier, n_lat - 1 + 2)

    def across(k):
        to = lax.rem(tile + k, n_lat)
        return pltpu.make_async_remote_copy(
            src_ref=send_ref.at[to],
            dst_ref=recv_ref.at[slab, tile],
            send_sem=send_sem.at[k],
            recv_sem=recv_sem.at[k],
            device_id=(to, slab),
            device_id_type=MESH,
        )

    def share(k, of, to, way):
        block = recv_ref.at[of, lax.rem(tile + n_lat - k, n_lat)]
        return pltpu.make_async_remote_copy(
            src_ref=block,
            dst_ref=block,
            send_sem=fwd_sem.at[way, k],
            recv_sem=got_sem.at[way, k],
            device_id=(tile, to),
            device_id_type=MESH,
        )

    def forward(k):
        share(k, slab, other, 0).start()
        share(k, slab, pair, 1).start()

    def relay(k):
        share(k, other, other, 0).wait_recv()
        share(k, other, pair, 2).start()

    @pl.loop(1, n_lat)
    def _(k):
        across(k).start()

    own = pltpu.make_async_copy(send_ref.at[tile], recv_ref.at[slab, tile], own_sem)
    own.start()
    own.wait()
    forward(0)

    @pl.loop(1, n_lat)
    def _(k):
        across(k).wait_recv()
        forward(k)
        relay(k - 1)

    relay(n_lat - 1)

    @pl.loop(0, n_lat)
    def _(k):
        share(k, pair, pair, 1).wait_recv()
        share(k, other + pair - slab, pair, 2).wait_recv()

    @pl.loop(1, n_lat)
    def _(k):
        across(k).wait_send()

    @pl.loop(0, n_lat)
    def _(k):
        share(k, slab, other, 0).wait_send()
        share(k, slab, pair, 1).wait_send()
        share(k, other, pair, 2).wait_send()


def sum_kernel(blocks, share, meta_ref, recv_ref, acc, todo):
    slab = lax.axis_index("rad")
    slots = blocks * share
    acc[...] = jnp.zeros(acc.shape, jnp.float32)
    lane = lax.broadcasted_iota(jnp.int32, (8, LANES), 1)
    sub = lax.broadcasted_iota(jnp.int32, (8, LANES), 0)
    ramp = 25 * sub + lane
    low = slab * CZ - 2 * HZ

    def listed(s, n):
        zb = meta_ref[slots + s] - low
        todo[n] = s
        return n + jnp.where((zb >= 0) & (zb < CZ + 3 * HZ), 1, 0)

    n = lax.fori_loop(0, slots, listed, 0, unroll=8)
    for more in range(SUM_UNROLL):
        todo[n + more] = 0

    def place(at, values, index, mask):
        for j in range(5):
            picked = jnp.where(mask, index + 5 * j, NGLL)
            for c in range(3):
                piece = jnp.take_along_axis(values[c], picked, axis=1, mode="promise_in_bounds")
                acc[pl.ds(pl.multiple_of(at + (3 * j + c) * 8, 8), 8), :] += piece

    def summed(step, _):
        later = []
        for u in range(SUM_UNROLL):
            s = todo[step * SUM_UNROLL + u]
            good = step * SUM_UNROLL + u < n
            x0 = jnp.clip(meta_ref[s], 0, CX - 5)
            zb = jnp.clip(meta_ref[slots + s] - low, 0, CZ + 3 * HZ - 1)
            y0 = jnp.clip(meta_ref[2 * slots + s], 0, NY - 5)
            block = lax.div(s, share)
            slot = s - block * share
            values = []
            for c in range(3):
                row = jnp.broadcast_to(recv_ref[block, pl.ds(c * share + slot, 1), :], (8, LANES))
                values.append(jnp.where(lane < NGLL, row, 0.0))
            half = lax.shift_right_logical(y0, 7)
            yl = y0 & (LANES - 1)
            index = ramp - (25 * x0 + yl)
            rows = (sub >= x0) & (sub < jnp.where(good, x0 + 5, 0))
            at = (half * ZP + zb) * 24
            place(at, values, index, rows & (lane >= yl) & (lane < yl + 5))
            later.append((at, values, index, rows, yl))
        widest = functools.reduce(jnp.maximum, [entry[4] for entry in later])

        @pl.when(widest > LANES - 5)
        def _():
            for at, values, index, rows, yl in later:
                over = rows & (lane < yl + 5 - LANES)

                @pl.when(yl > LANES - 5)
                def _():
                    place(at + ZP * 24, values, index + LANES, over)

        return 0

    lax.fori_loop(0, lax.div(n + SUM_UNROLL - 1, SUM_UNROLL), summed, 0)


def finish_kernel(n_lat, taps_ref, wx_ref, acc, wy_ref, out_ref, planes, rows_ref, send_sem, recv_sem):
    tile, slab = lax.axis_index("lat"), lax.axis_index("rad")
    barrier = pltpu.get_barrier_semaphore()
    has_prev, has_next = tile > 0, tile < n_lat - 1
    halo = HW * CZ

    @pl.when(has_prev)
    def _():
        pl.semaphore_signal(barrier, inc=1, device_id=(tile - 1, slab), device_id_type=MESH)

    @pl.when(has_next)
    def _():
        pl.semaphore_signal(barrier, inc=1, device_id=(tile + 1, slab), device_id_type=MESH)

    def at(c, row, count):
        return rows_ref.at[:, pl.ds(c * PADX * CZ + row, count), :]

    def to_next(c):
        return pltpu.make_async_remote_copy(
            src_ref=at(c, CX * CZ, halo),
            dst_ref=at(c, 0, halo),
            send_sem=send_sem.at[0, c],
            recv_sem=recv_sem.at[0, c],
            device_id=(tile + 1, slab),
            device_id_type=MESH,
        )

    def to_prev(c):
        return pltpu.make_async_remote_copy(
            src_ref=at(c, halo, halo),
            dst_ref=at(c, halo + CX * CZ, halo),
            send_sem=send_sem.at[1, c],
            recv_sem=recv_sem.at[1, c],
            device_id=(tile - 1, slab),
            device_id_type=MESH,
        )

    for c in range(3):

        @pl.loop(0, CZ, unroll=4)
        def _(z):
            for half in range(NY // LANES):
                total = jnp.zeros((CX, LANES), jnp.float32)
                for d in range(TAPS):
                    weight = taps_ref[(slab * CZ + z) * TAPS + d]
                    row = pl.multiple_of(((half * ZP + z + HZ + d) * 3 + c) * CX, 8)
                    total = total + weight * acc[pl.ds(row, CX), :]
                cols = slice(half * LANES, (half + 1) * LANES)
                planes[pl.ds(pl.multiple_of(z * CX, 8), CX), cols] = total

        product = jnp.dot(planes[...], wy_ref[...], precision=lax.Precision.HIGHEST)
        for z in range(CZ):
            for half in range(NY // LANES):
                piece = product[z * CX : (z + 1) * CX, half * LANES : (half + 1) * LANES]
                rows_ref[half, pl.ds(c * PADX * CZ + halo + z, CX, stride=CZ), :] = piece

        if c == 0:
            beside = jnp.minimum(tile, 1) + jnp.minimum(n_lat - 1 - tile, 1)
            pl.semaphore_wait(barrier, beside)

        @pl.when(has_next)
        def _():
            to_next(c).start()

        @pl.when(has_prev)
        def _():
            to_prev(c).start()

        zeros = jnp.zeros((NY // LANES, halo, LANES), jnp.float32)

        @pl.when(tile == 0)
        def _():
            rows_ref[:, c * PADX * CZ : c * PADX * CZ + halo, :] = zeros

        @pl.when(tile == n_lat - 1)
        def _():
            rows_ref[:, c * PADX * CZ + halo + CX * CZ : (c + 1) * PADX * CZ, :] = zeros

    for c in range(3):

        @pl.when(has_prev)
        def _():
            to_next(c).wait_recv()

        @pl.when(has_next)
        def _():
            to_prev(c).wait_recv()

        @pl.loop(0, CX)
        def _(x):
            for half in range(NY // LANES):
                total = jnp.zeros((CZ, LANES), jnp.float32)
                for d in range(2 * HW + 1):
                    row = pl.multiple_of(c * PADX * CZ + (x + d) * CZ, 8)
                    total = total + wx_ref[x * (2 * HW + 1) + d] * rows_ref[half, pl.ds(row, CZ), :]
                out_ref[c, x, :, half * LANES : (half + 1) * LANES] = total

    for c in range(3):

        @pl.when(has_next)
        def _():
            to_next(c).wait_send()

        @pl.when(has_prev)
        def _():
            to_prev(c).wait_send()


def x_weights(width_class, n_lat):
    rows = lax.axis_index("lat") * CX + jnp.arange(CX)
    sigma = 1.0 + 0.75 * width_class[0].astype(jnp.float32)
    offsets = jnp.arange(-HW, HW + 1)
    target = rows[:, None] + offsets[None, :]
    valid = (target >= 0) & (target < CX * n_lat)
    gauss = jnp.exp(-(offsets[None, :].astype(jnp.float32) ** 2) / (2.0 * sigma**2))
    gauss = jnp.where(valid, gauss, 0.0)
    return gauss / jnp.sum(gauss, axis=1, keepdims=True)


def on_device(n_lat, n_rad, kernels, cells, tiles, width_class):
    elements = tiles.shape[0]
    cap = max(2, 2 * elements // n_lat)
    share = -(-cap // n_rad)
    blocks = n_rad * n_lat
    slots = blocks * share
    params = pltpu.CompilerParams(vmem_limit_bytes=VMEM_LIMIT)
    smem = pl.BlockSpec(memory_space=pltpu.SMEM)
    vmem = pl.BlockSpec(memory_space=pltpu.VMEM)
    send = pl.pallas_call(
        functools.partial(pack_kernel, n_lat, n_rad, share, elements),
        out_shape=jax.ShapeDtypeStruct((n_lat + 1, 3 * share, LANES), jnp.float32),
        in_specs=[smem, smem, vmem],
        out_specs=vmem,
        scratch_shapes=[
            pltpu.SMEM((n_lat,), jnp.int32),
            pltpu.SMEM((elements + PACK_UNROLL,), jnp.int32),
            pltpu.SMEM((elements + PACK_UNROLL,), jnp.int32),
        ],
        compiler_params=params,
    )(tiles.reshape(-1), cells, kernels)
    recv = pl.pallas_call(
        functools.partial(exchange_kernel, n_lat, n_rad),
        out_shape=jax.ShapeDtypeStruct((n_rad, n_lat, 3 * share, LANES), jnp.float32),
        in_specs=[vmem],
        out_specs=vmem,
        scratch_shapes=[
            pltpu.SemaphoreType.DMA,
            pltpu.SemaphoreType.DMA((n_lat,)),
            pltpu.SemaphoreType.DMA((n_lat,)),
            pltpu.SemaphoreType.DMA((3, n_lat)),
            pltpu.SemaphoreType.DMA((3, n_lat)),
        ],
        compiler_params=pltpu.CompilerParams(
            vmem_limit_bytes=VMEM_LIMIT, collective_id=0, has_side_effects=True
        ),
    )(send)
    recv = recv.reshape(blocks, 3 * share, LANES)
    meta = recv[:, :share, NGLL:].transpose(2, 0, 1).reshape(-1).astype(jnp.int32)
    grid_rows = NY // LANES * ZP * 24
    summed = pl.pallas_call(
        functools.partial(sum_kernel, blocks, share),
        out_shape=jax.ShapeDtypeStruct((grid_rows, LANES), jnp.float32),
        in_specs=[smem, vmem],
        out_specs=vmem,
        scratch_shapes=[pltpu.SMEM((slots + SUM_UNROLL,), jnp.int32)],
        compiler_params=params,
    )(meta, recv)
    return pl.pallas_call(
        functools.partial(finish_kernel, n_lat),
        out_shape=jax.ShapeDtypeStruct((3, CX, CZ, NY), jnp.float32),
        in_specs=[smem, smem, vmem, vmem],
        out_specs=vmem,
        scratch_shapes=[
            pltpu.VMEM((CZ * CX, NY), jnp.float32),
            pltpu.VMEM((NY // LANES, 3 * PADX * CZ, LANES), jnp.float32),
            pltpu.SemaphoreType.DMA((2, 3)),
            pltpu.SemaphoreType.DMA((2, 3)),
        ],
        compiler_params=pltpu.CompilerParams(
            vmem_limit_bytes=VMEM_LIMIT, collective_id=1, has_side_effects=True
        ),
    )(
        jnp.asarray(z_taps(n_rad).reshape(-1)),
        x_weights(width_class, n_lat).reshape(-1),
        summed,
        jnp.asarray(band_matrix(NY, 2.5, HY).T.astype(np.float32)),
    )


def solution(mesh):
    return jax.shard_map(
        functools.partial(on_device, mesh.shape["lat"], mesh.shape["rad"]),
        mesh=mesh,
        in_specs=(P(None, "lat"), P(None, "lat"), P("lat", None), P("lat")),
        out_specs=P(None, "lat", "rad", None),
        check_vma=False,
    )
```

```python
import functools

import jax
import jax.numpy as jnp
import numpy as np
from jax import lax
from jax.experimental import pallas as pl
from jax.experimental.pallas import tpu as pltpu
from jax.sharding import PartitionSpec as P

CX = 8
NY = 256
CZ = 32
NGLL = 125
HW = 4
HY = 8
HZ = 4
ZP = CZ + 4 * HZ
LANES = 128
TAPS = 2 * HZ + 1
PADX = CX + 2 * HW
PACK_UNROLL = 4
SUM_UNROLL = 4
VMEM_LIMIT = 48 * 2**20
MESH = pl.DeviceIdType.MESH


def band_matrix(count, sigma, half):
    place = np.arange(count)
    gap = place[None, :] - place[:, None]
    gauss = np.where(np.abs(gap) <= half, np.exp(-(gap**2) / (2.0 * sigma**2)), 0.0)
    return gauss / gauss.sum(axis=1, keepdims=True)


def z_taps(n_rad):
    full = np.pad(band_matrix(CZ * n_rad, 1.5, HZ), ((0, 0), (HZ, HZ)))
    return np.stack([full[z, z : z + TAPS] for z in range(CZ * n_rad)]).astype(np.float32)


def pack_kernel(
    n_lat, n_rad, share, elements, tiles_ref, cells_hbm, kern_hbm, out_ref, count, todo, place, cells_ref, kern_ref, sems
):
    slab = lax.axis_index("rad")
    rows = elements * NGLL // LANES
    bring_cells = pltpu.make_async_copy(cells_hbm, cells_ref, sems.at[0])
    bring_kern = pltpu.make_async_copy(kern_hbm, kern_ref, sems.at[1])
    bring_cells.start()
    bring_kern.start()
    out_ref[...] = jnp.full(out_ref.shape, -1000.0, jnp.float32)
    lane = lax.broadcasted_iota(jnp.int32, (3, LANES), 1)

    @pl.loop(0, n_lat)
    def _(t):
        count[t] = 0

    def listed(e, n):
        t = tiles_ref[e]
        rank = count[t]
        count[t] = rank + 1
        slot = lax.div(rank, n_rad)
        todo[n] = e
        place[n] = t * share + slot
        return n + jnp.where(rank - slot * n_rad == slab, 1, 0)

    n = lax.fori_loop(0, elements, listed, 0, unroll=4)
    for more in range(PACK_UNROLL):
        todo[n + more] = 0
        place[n + more] = n_lat * share
    bring_cells.wait()
    bring_kern.wait()

    def packed(step, _):
        for u in range(PACK_UNROLL):
            e = todo[step * PACK_UNROLL + u]
            at = place[step * PACK_UNROLL + u]
            start = e * NGLL
            row = lax.shift_right_logical(start, 7)
            off = start & (LANES - 1)
            after = jnp.minimum(row + 1, rows - 1)
            a = kern_ref[:, pl.ds(pl.multiple_of(row * LANES, LANES), LANES)]
            b = kern_ref[:, pl.ds(pl.multiple_of(after * LANES, LANES), LANES)]
            v = pltpu.roll(jnp.where(lane >= off, a, b), (LANES - off) & (LANES - 1), 1)
            v = jnp.where(lane == NGLL, cells_ref[0, e].astype(jnp.float32), v)
            v = jnp.where(lane == NGLL + 1, cells_ref[1, e].astype(jnp.float32), v)
            v = jnp.where(lane == NGLL + 2, cells_ref[2, e].astype(jnp.float32), v)
            t = lax.div(at, share)
            slot = at - t * share
            for c in range(3):
                out_ref[t, pl.ds(c * share + slot, 1), :] = v[c : c + 1]
        return 0

    lax.fori_loop(0, lax.div(n + PACK_UNROLL - 1, PACK_UNROLL), packed, 0)


def exchange_kernel(n_lat, n_rad, send_ref, recv_ref, own_sem, send_sem, recv_sem, fwd_sem, got_sem):
    tile, slab = lax.axis_index("lat"), lax.axis_index("rad")
    barrier = pltpu.get_barrier_semaphore()

    @pl.loop(1, n_lat)
    def _(k):
        pl.semaphore_signal(barrier, inc=1, device_id=(lax.rem(tile + k, n_lat), slab), device_id_type=MESH)

    pair = slab + 1 - 2 * lax.rem(slab, 2)
    other = slab + 2 - 4 * lax.div(slab, 2)
    for peer in (pair, other):
        pl.semaphore_signal(barrier, inc=1, device_id=(tile, peer), device_id_type=MESH)
    pl.semaphore_wait(barrier, n_lat - 1 + 2)

    def across(k):
        to = lax.rem(tile + k, n_lat)
        return pltpu.make_async_remote_copy(
            src_ref=send_ref.at[to],
            dst_ref=recv_ref.at[slab, tile],
            send_sem=send_sem.at[k],
            recv_sem=recv_sem.at[k],
            device_id=(to, slab),
            device_id_type=MESH,
        )

    def share(k, of, to, way):
        block = recv_ref.at[of, lax.rem(tile + n_lat - k, n_lat)]
        return pltpu.make_async_remote_copy(
            src_ref=block,
            dst_ref=block,
            send_sem=fwd_sem.at[way, k],
            recv_sem=got_sem.at[way, k],
            device_id=(tile, to),
            device_id_type=MESH,
        )

    def forward(k):
        share(k, slab, other, 0).start()
        share(k, slab, pair, 1).start()

    def relay(k):
        share(k, other, other, 0).wait_recv()
        share(k, other, pair, 2).start()

    @pl.loop(1, n_lat)
    def _(k):
        across(k).start()

    own = pltpu.make_async_copy(send_ref.at[tile], recv_ref.at[slab, tile], own_sem)
    own.start()
    own.wait()
    forward(0)

    @pl.loop(1, n_lat)
    def _(k):
        across(k).wait_recv()
        forward(k)

    @pl.loop(0, n_lat)
    def _(k):
        relay(k)

    @pl.loop(0, n_lat)
    def _(k):
        share(k, pair, pair, 1).wait_recv()
        share(k, other + pair - slab, pair, 2).wait_recv()

    @pl.loop(1, n_lat)
    def _(k):
        across(k).wait_send()

    @pl.loop(0, n_lat)
    def _(k):
        share(k, slab, other, 0).wait_send()
        share(k, slab, pair, 1).wait_send()
        share(k, other, pair, 2).wait_send()


def sum_kernel(blocks, share, meta_ref, recv_ref, acc, todo):
    slab = lax.axis_index("rad")
    slots = blocks * share
    acc[...] = jnp.zeros(acc.shape, jnp.float32)
    lane = lax.broadcasted_iota(jnp.int32, (8, LANES), 1)
    sub = lax.broadcasted_iota(jnp.int32, (8, LANES), 0)
    ramp = 25 * sub + lane
    low = slab * CZ - 2 * HZ

    def listed(s, n):
        zb = meta_ref[slots + s] - low
        todo[n] = s
        return n + jnp.where((zb >= 0) & (zb < CZ + 3 * HZ), 1, 0)

    n = lax.fori_loop(0, slots, listed, 0, unroll=8)
    for more in range(SUM_UNROLL):
        todo[n + more] = 0

    def place(at, values, index, mask):
        for j in range(5):
            picked = jnp.where(mask, index + 5 * j, NGLL)
            for c in range(3):
                piece = jnp.take_along_axis(values[c], picked, axis=1, mode="promise_in_bounds")
                acc[pl.ds(pl.multiple_of(at + (3 * j + c) * 8, 8), 8), :] += piece

    def summed(step, _):
        later = []
        for u in range(SUM_UNROLL):
            s = todo[step * SUM_UNROLL + u]
            good = step * SUM_UNROLL + u < n
            x0 = jnp.clip(meta_ref[s], 0, CX - 5)
            zb = jnp.clip(meta_ref[slots + s] - low, 0, CZ + 3 * HZ - 1)
            y0 = jnp.clip(meta_ref[2 * slots + s], 0, NY - 5)
            block = lax.div(s, share)
            slot = s - block * share
            values = []
            for c in range(3):
                row = jnp.broadcast_to(recv_ref[block, pl.ds(c * share + slot, 1), :], (8, LANES))
                values.append(jnp.where(lane < NGLL, row, 0.0))
            half = lax.shift_right_logical(y0, 7)
            yl = y0 & (LANES - 1)
            index = ramp - (25 * x0 + yl)
            rows = (sub >= x0) & (sub < jnp.where(good, x0 + 5, 0))
            at = (half * ZP + zb) * 24
            place(at, values, index, rows & (lane >= yl) & (lane < yl + 5))
            later.append((at, values, index, rows, yl))
        widest = functools.reduce(jnp.maximum, [entry[4] for entry in later])

        @pl.when(widest > LANES - 5)
        def _():
            for at, values, index, rows, yl in later:
                over = rows & (lane < yl + 5 - LANES)

                @pl.when(yl > LANES - 5)
                def _():
                    place(at + ZP * 24, values, index + LANES, over)

        return 0

    lax.fori_loop(0, lax.div(n + SUM_UNROLL - 1, SUM_UNROLL), summed, 0)


def finish_kernel(n_lat, taps_ref, wx_ref, acc, wy_ref, out_ref, planes, rows_ref, send_sem, recv_sem):
    tile, slab = lax.axis_index("lat"), lax.axis_index("rad")
    barrier = pltpu.get_barrier_semaphore()
    has_prev, has_next = tile > 0, tile < n_lat - 1
    halo = HW * CZ

    @pl.when(has_prev)
    def _():
        pl.semaphore_signal(barrier, inc=1, device_id=(tile - 1, slab), device_id_type=MESH)

    @pl.when(has_next)
    def _():
        pl.semaphore_signal(barrier, inc=1, device_id=(tile + 1, slab), device_id_type=MESH)

    def at(c, row, count):
        return rows_ref.at[:, pl.ds(c * PADX * CZ + row, count), :]

    def to_next(c):
        return pltpu.make_async_remote_copy(
            src_ref=at(c, CX * CZ, halo),
            dst_ref=at(c, 0, halo),
            send_sem=send_sem.at[0, c],
            recv_sem=recv_sem.at[0, c],
            device_id=(tile + 1, slab),
            device_id_type=MESH,
        )

    def to_prev(c):
        return pltpu.make_async_remote_copy(
            src_ref=at(c, halo, halo),
            dst_ref=at(c, halo + CX * CZ, halo),
            send_sem=send_sem.at[1, c],
            recv_sem=recv_sem.at[1, c],
            device_id=(tile - 1, slab),
            device_id_type=MESH,
        )

    for c in range(3):

        @pl.loop(0, CZ, unroll=4)
        def _(z):
            for half in range(NY // LANES):
                total = jnp.zeros((CX, LANES), jnp.float32)
                for d in range(TAPS):
                    weight = taps_ref[(slab * CZ + z) * TAPS + d]
                    row = pl.multiple_of(((half * ZP + z + HZ + d) * 3 + c) * CX, 8)
                    total = total + weight * acc[pl.ds(row, CX), :]
                cols = slice(half * LANES, (half + 1) * LANES)
                planes[pl.ds(pl.multiple_of(z * CX, 8), CX), cols] = total

        product = jnp.dot(planes[...], wy_ref[...], precision=lax.Precision.HIGHEST)
        for z in range(CZ):
            for half in range(NY // LANES):
                piece = product[z * CX : (z + 1) * CX, half * LANES : (half + 1) * LANES]
                rows_ref[half, pl.ds(c * PADX * CZ + halo + z, CX, stride=CZ), :] = piece

        if c == 0:
            beside = jnp.minimum(tile, 1) + jnp.minimum(n_lat - 1 - tile, 1)
            pl.semaphore_wait(barrier, beside)

        @pl.when(has_next)
        def _():
            to_next(c).start()

        @pl.when(has_prev)
        def _():
            to_prev(c).start()

        zeros = jnp.zeros((NY // LANES, halo, LANES), jnp.float32)

        @pl.when(tile == 0)
        def _():
            rows_ref[:, c * PADX * CZ : c * PADX * CZ + halo, :] = zeros

        @pl.when(tile == n_lat - 1)
        def _():
            rows_ref[:, c * PADX * CZ + halo + CX * CZ : (c + 1) * PADX * CZ, :] = zeros

    for c in range(3):

        @pl.when(has_prev)
        def _():
            to_next(c).wait_recv()

        @pl.when(has_next)
        def _():
            to_prev(c).wait_recv()

        @pl.loop(0, CX)
        def _(x):
            for half in range(NY // LANES):
                total = jnp.zeros((CZ, LANES), jnp.float32)
                for d in range(2 * HW + 1):
                    row = pl.multiple_of(c * PADX * CZ + (x + d) * CZ, 8)
                    total = total + wx_ref[x * (2 * HW + 1) + d] * rows_ref[half, pl.ds(row, CZ), :]
                out_ref[c, x, :, half * LANES : (half + 1) * LANES] = total

    for c in range(3):

        @pl.when(has_next)
        def _():
            to_next(c).wait_send()

        @pl.when(has_prev)
        def _():
            to_prev(c).wait_send()


def x_weights(width_class, n_lat):
    rows = lax.axis_index("lat") * CX + jnp.arange(CX)
    sigma = 1.0 + 0.75 * width_class[0].astype(jnp.float32)
    offsets = jnp.arange(-HW, HW + 1)
    target = rows[:, None] + offsets[None, :]
    valid = (target >= 0) & (target < CX * n_lat)
    gauss = jnp.exp(-(offsets[None, :].astype(jnp.float32) ** 2) / (2.0 * sigma**2))
    gauss = jnp.where(valid, gauss, 0.0)
    return gauss / jnp.sum(gauss, axis=1, keepdims=True)


def on_device(n_lat, n_rad, kernels, cells, tiles, width_class):
    elements = tiles.shape[0]
    cap = max(2, 2 * elements // n_lat)
    share = -(-cap // n_rad)
    blocks = n_rad * n_lat
    slots = blocks * share
    params = pltpu.CompilerParams(vmem_limit_bytes=VMEM_LIMIT)
    smem = pl.BlockSpec(memory_space=pltpu.SMEM)
    vmem = pl.BlockSpec(memory_space=pltpu.VMEM)
    hbm = pl.BlockSpec(memory_space=pl.ANY)
    send = pl.pallas_call(
        functools.partial(pack_kernel, n_lat, n_rad, share, elements),
        out_shape=jax.ShapeDtypeStruct((n_lat + 1, 3 * share, LANES), jnp.float32),
        in_specs=[smem, hbm, hbm],
        out_specs=vmem,
        scratch_shapes=[
            pltpu.SMEM((n_lat,), jnp.int32),
            pltpu.SMEM((elements + PACK_UNROLL,), jnp.int32),
            pltpu.SMEM((elements + PACK_UNROLL,), jnp.int32),
            pltpu.SMEM(cells.shape, jnp.int32),
            pltpu.VMEM(kernels.shape, jnp.float32),
            pltpu.SemaphoreType.DMA((2,)),
        ],
        compiler_params=params,
    )(tiles.reshape(-1), cells, kernels)
    recv = pl.pallas_call(
        functools.partial(exchange_kernel, n_lat, n_rad),
        out_shape=jax.ShapeDtypeStruct((n_rad, n_lat, 3 * share, LANES), jnp.float32),
        in_specs=[vmem],
        out_specs=vmem,
        scratch_shapes=[
            pltpu.SemaphoreType.DMA,
            pltpu.SemaphoreType.DMA((n_lat,)),
            pltpu.SemaphoreType.DMA((n_lat,)),
            pltpu.SemaphoreType.DMA((3, n_lat)),
            pltpu.SemaphoreType.DMA((3, n_lat)),
        ],
        compiler_params=pltpu.CompilerParams(
            vmem_limit_bytes=VMEM_LIMIT, collective_id=0, has_side_effects=True
        ),
    )(send)
    recv = recv.reshape(blocks, 3 * share, LANES)
    meta = recv[:, :share, NGLL:].transpose(2, 0, 1).reshape(-1).astype(jnp.int32)
    grid_rows = NY // LANES * ZP * 24
    summed = pl.pallas_call(
        functools.partial(sum_kernel, blocks, share),
        out_shape=jax.ShapeDtypeStruct((grid_rows, LANES), jnp.float32),
        in_specs=[smem, vmem],
        out_specs=vmem,
        scratch_shapes=[pltpu.SMEM((slots + SUM_UNROLL,), jnp.int32)],
        compiler_params=params,
    )(meta, recv)
    return pl.pallas_call(
        functools.partial(finish_kernel, n_lat),
        out_shape=jax.ShapeDtypeStruct((3, CX, CZ, NY), jnp.float32),
        in_specs=[smem, smem, vmem, vmem],
        out_specs=vmem,
        scratch_shapes=[
            pltpu.VMEM((CZ * CX, NY), jnp.float32),
            pltpu.VMEM((NY // LANES, 3 * PADX * CZ, LANES), jnp.float32),
            pltpu.SemaphoreType.DMA((2, 3)),
            pltpu.SemaphoreType.DMA((2, 3)),
        ],
        compiler_params=pltpu.CompilerParams(
            vmem_limit_bytes=VMEM_LIMIT, collective_id=1, has_side_effects=True
        ),
    )(
        jnp.asarray(z_taps(n_rad).reshape(-1)),
        x_weights(width_class, n_lat).reshape(-1),
        summed,
        jnp.asarray(band_matrix(NY, 2.5, HY).T.astype(np.float32)),
    )


def solution(mesh):
    return jax.shard_map(
        functools.partial(on_device, mesh.shape["lat"], mesh.shape["rad"]),
        mesh=mesh,
        in_specs=(P(None, "lat"), P(None, "lat"), P("lat", None), P("lat")),
        out_specs=P(None, "lat", "rad", None),
        check_vma=False,
    )
```
